512 devices in a mesh: side: 2 (over y_lo), gx: 32 (over y_hi, z), gy: 8 (over x, core).
Axes of the slice: x: 4, y: 4 (y_hi: 2, y_lo: 2; y = y_hi * 2 + y_lo), z: 16, core: 2. Of those that a mesh axis runs over, the one named last changes fastest.
Arguments:
- hidden_in: bfloat16 [32, 2, 8192], P(None, None, ('side', 'gx')), may hold values from -10 to 10
- queries: bfloat16 [32, 2, 64, 128], P('gx', None, 'gy'), may hold values from -110 to 110
- kv_cache: bfloat16 [32, 2048, 8, 256], P('gx', 'side', 'gy'), may hold values from -6 to 6
- new_kv: bfloat16 [32, 2, 8, 256], P('gx', None, 'gy'), may hold values from -5 to 5
- lengths: int32 [32], P('gx'), may hold values from 256 to 2048
- out_weight: bfloat16 [8192, 8192], P('gy', ('side', 'gx')), may hold values from -1 to 1
- norm_gain: float32 [8192], P(('side', 'gx')), may hold values from 0.5 to 1.5
- gate_weight: bfloat16 [8192, 28672], P(('side', 'gx'), 'gy'), may hold values from -0.0625 to 0.0625
- up_weight: bfloat16 [8192, 28672], P(('side', 'gx'), 'gy'), may hold values from -0.0625 to 0.0625
- down_weight: bfloat16 [28672, 8192], P('gy', ('side', 'gx')), may hold values from -0.03125 to 0.03125
Outputs:
- hidden_out: bfloat16 [32, 2, 8192], P(None, None, ('side', 'gx'))
The draws below stay inside these ranges and needn't reach their ends.
All inputs are finite; a program needn't handle non-finite values.
Results may differ from the reference program's by a relative error of at most 0.014.
Values may be sent and summed in bfloat16 or wider, within the bound.
No kernel may reach another device: no remote copies, remote signals or barrier semaphores. Data moves between devices by JAX's collectives and lax.ppermute only.
A program may use at most 64 MiB of HBM per device.

```python
import math
import jax
import jax.numpy as jnp
from jax import lax

D = 8192
FF = 28672
HEADS = 64
KVH = 8
HD = 128
CTX = 2048
REQS = 32


def leading_keys(key):
    raw = jax.random.normal(jax.random.fold_in(key, 99), (REQS, 2, KVH, HD), jnp.float32)
    return jnp.clip(raw, -5.0, 5.0)


def fresh_keys(key):
    raw = jax.random.normal(jax.random.fold_in(key, 97), (REQS, 2, KVH, HD), jnp.float32)
    return jnp.clip(raw, -5.0, 5.0)


def offset_signs(key):
    flips = jax.random.bernoulli(jax.random.fold_in(key, 96), 0.5, (KVH, HD))
    return jnp.where(flips, 1.0, -1.0)


def width_ramp():
    return 0.5 + 1.5 * lax.iota(jnp.int32, D).astype(jnp.float32) / D


def column_pattern(key):
    flips = jax.random.bernoulli(jax.random.fold_in(key, 95), 0.5, (D,))
    return jnp.where(flips, 1.0, -1.0) * width_ramp()


def value_offsets(signs, lowest):
    ramp = lax.iota(jnp.int32, CTX).astype(jnp.float32) / (CTX - 1)
    level = lowest + (3.0 - lowest) * ramp
    return signs[None, None, :, :] * level[None, :, None, None]


def draw_kv_cache(key, part):
    leading = leading_keys(key)
    signs = offset_signs(key)
    key = jax.random.fold_in(key, 11)
    keys_part = jnp.clip(jax.random.normal(key, (REQS, CTX, KVH, HD), jnp.float32), -5.0, 5.0)
    noise = jnp.clip(jax.random.normal(jax.random.fold_in(key, 3), (REQS, CTX, KVH, HD), jnp.float32), -3.0, 3.0)
    second = leading[:, 1]
    offsets = value_offsets(signs, 0.5)
    front = jnp.stack([leading[:, 0], second], axis=1)
    keys_part = keys_part.at[:, 0:2].set(front)
    filled = jnp.concatenate([keys_part, noise + offsets], axis=3)
    return filled.astype(jnp.bfloat16)


def draw_new_kv(key, part):
    keys_part = fresh_keys(key)
    key = jax.random.fold_in(key, 15)
    values = jnp.clip(jax.random.normal(key, (REQS, 2, KVH, HD), jnp.float32), -5.0, 5.0)
    return jnp.concatenate([keys_part, values], axis=3).astype(jnp.bfloat16)


def draw_queries(key, part):
    fresh = fresh_keys(key)
    key = jax.random.fold_in(key, 12)
    group = HEADS // KVH
    drawn = jnp.clip(jax.random.normal(key, (REQS, 2, HEADS, HD), jnp.float32), -5.0, 5.0)
    toward = jnp.repeat(fresh, group, axis=2)
    pull = jax.random.uniform(jax.random.fold_in(key, 8), (REQS, 1, HEADS, 1), jnp.float32, 0.1, 0.8)
    drawn = drawn + pull * toward
    return drawn.astype(jnp.bfloat16)


def draw_out_weight(key, part):
    signs = offset_signs(key)
    pattern = column_pattern(key)
    key = jax.random.fold_in(key, 16)
    width = HEADS * HD
    rows = jnp.repeat(signs, HEADS // KVH, axis=0).reshape(width)
    drawn = jnp.clip(jax.random.normal(key, (width, D), jnp.float32), -4.0, 4.0) / math.sqrt(width)
    common = 1.5 / width * rows[:, None] * pattern[None, :]
    return (drawn + common).astype(jnp.bfloat16)


def draw_hidden_in(key, part):
    pattern = column_pattern(key)
    key = jax.random.fold_in(key, 13)
    columns = width_ramp()
    base = jnp.clip(jax.random.normal(key, (REQS, 2, D), jnp.float32), -5.0, 5.0)
    mixed = base * columns + 0.5 * pattern
    return jnp.clip(mixed, -10.0, 10.0).astype(jnp.bfloat16)


def draw_lengths(key, part):
    key = jax.random.fold_in(key, 14)
    raw = jax.random.randint(key, (REQS,), CTX // 8, CTX + 1)
    longest = jax.random.randint(jax.random.fold_in(key, 6), (), 0, REQS)
    return jnp.where(lax.iota(jnp.int32, REQS) == longest, CTX, raw).astype(jnp.int32)


def levels(rng, extent, split, least, high):
    loudness, own = 1.0, jax.random.fold_in(rng, 6)
    for dim, blocks in split:
        heights = jnp.exp(jax.random.uniform(jax.random.fold_in(own, dim), (blocks,), jnp.float32, least / len(split), high / len(split)))
        loudness = loudness * jnp.repeat(heights, extent[dim] // blocks).reshape([-1 if axis == dim else 1 for axis in range(len(extent))])
    return loudness


def normal_values(key, dims, scale, bound, shards=(), held_as=jnp.bfloat16):
    values = jax.random.normal(key, dims, jnp.float32) * scale
    if len(shards) > 0:
        values = levels(key, dims, shards, -0.22, 0.18) * values
    return jnp.clip(values, min=-bound, max=bound).astype(held_as)


def setup_inputs(seed: int = 0) -> dict:
    arg_keys = jax.random.split(jax.random.key(seed), 11)
    return {
        "hidden_in": draw_hidden_in(jax.random.fold_in(arg_keys[10], 71), 0),
        "queries": draw_queries(jax.random.fold_in(arg_keys[10], 71), 0),
        "kv_cache": draw_kv_cache(jax.random.fold_in(arg_keys[10], 71), 0),
        "new_kv": draw_new_kv(jax.random.fold_in(arg_keys[10], 71), 0),
        "lengths": draw_lengths(jax.random.fold_in(arg_keys[10], 71), 0),
        "out_weight": draw_out_weight(jax.random.fold_in(arg_keys[10], 71), 0),
        "norm_gain": jnp.clip(1.0 + 0.1 * jax.random.normal(arg_keys[6], (D,), jnp.float32), 0.5, 1.5),
        "gate_weight": normal_values(arg_keys[7], (D, FF), D ** -0.5, 0.0625, ((0, 64), (1, 8))),
        "up_weight": normal_values(arg_keys[8], (D, FF), D ** -0.5, 0.0625, ((0, 64), (1, 8))),
        "down_weight": normal_values(arg_keys[9], (FF, D), FF ** -0.5, 0.03125, ((0, 8), (1, 64))),
    }


big_negative = -1e+30

def attend_one(items):
    query, cache, fresh, length = items
    group = HEADS // KVH
    keys = jnp.concatenate([cache[:, :, :HD], fresh[:, :, :HD]], axis=0).astype(jnp.float32)
    values = jnp.concatenate([cache[:, :, HD:], fresh[:, :, HD:]], axis=0).astype(jnp.float32)
    grouped = query.astype(jnp.float32).reshape(2, KVH, group, HD)
    scores = jnp.einsum('tgid,cgd->tgic', grouped, keys) / math.sqrt(HD)
    position = lax.iota(jnp.int32, CTX + 2)
    draft = lax.iota(jnp.int32, 2)
    usable = jnp.where(position[None, :] < CTX, position[None, :] < length, position[None, :] - CTX <= draft[:, None])
    usable = usable[:, None, None, :]
    peak = lax.optimization_barrier(jnp.max(jnp.where(usable, scores, big_negative), axis=-1, keepdims=True))
    weights = jnp.where(usable, jnp.exp(scores - peak), 0.0)
    total = lax.optimization_barrier(jnp.sum(weights, axis=-1, keepdims=True))
    rounded = lax.optimization_barrier(weights.astype(jnp.bfloat16)).astype(jnp.float32)
    mixed = jnp.einsum('tgic,cgd->tgid', rounded, values) / total
    return mixed.astype(jnp.bfloat16).reshape(2, HEADS * HD)

def reference(hidden_in, queries, kv_cache, new_kv, lengths, out_weight, norm_gain, gate_weight, up_weight, down_weight):
    attended = lax.map(attend_one, (queries, kv_cache, new_kv, lengths))
    attended = attended.reshape(REQS * 2, HEADS * HD)
    middle = hidden_in.reshape(REQS * 2, D).astype(jnp.float32) + jnp.dot(attended, out_weight, preferred_element_type=jnp.float32)
    mean_square = lax.optimization_barrier(jnp.mean(middle * middle, axis=1, keepdims=True))
    normed = (middle * lax.rsqrt(mean_square + 1e-05) * norm_gain).astype(jnp.bfloat16)
    gate = jnp.dot(normed, gate_weight, preferred_element_type=jnp.float32)
    upper = jnp.dot(normed, up_weight, preferred_element_type=jnp.float32)
    activated = (jax.nn.silu(gate) * upper).astype(jnp.bfloat16)
    result = middle + jnp.dot(activated, down_weight, preferred_element_type=jnp.float32)
    return result.astype(jnp.bfloat16).reshape(REQS, 2, D)
```

```python
import math

import jax
import jax.numpy as jnp
from jax import lax
from jax.sharding import Mesh, PartitionSpec as P

D = 8192
big_negative = -1e30
bf16 = jnp.bfloat16
f32 = jnp.float32

SIDES, YHI, ZS = 2, 2, 16
YS = SIDES * YHI
ROWS = ("side", "yhi", "z")
Y = ("side", "yhi")
GY = ("x", "core")


def spread(value, axes, count):
    return lax.all_to_all(jnp.broadcast_to(value, (count, *value.shape)), axes, 0, 0)


def partial_attention(queries, kv_cache, new_kv, lengths, side_index, last_side):
    half, doubled = kv_cache.shape[1], kv_cache.shape[3]
    head = doubled // 2
    group = queries.shape[2]
    query = queries.reshape(2 * group, head)
    cache, fresh = kv_cache[0, :, 0], new_kv[0, :, 0]
    scale = 1.0 / math.sqrt(head)
    contract_last = (((1,), (1,)), ((), ()))
    scores = lax.dot_general(query, cache[:, :head], contract_last, preferred_element_type=f32) * scale
    usable = (side_index * half + lax.iota(jnp.int32, half) < lengths[0])[None, :]
    draft = lax.iota(jnp.int32, 2 * group) // group
    seen = (lax.iota(jnp.int32, 2)[None, :] <= draft[:, None]) & last_side
    new_scores = lax.dot_general(query, fresh[:, :head], contract_last, preferred_element_type=f32) * scale
    scores = jnp.where(usable, scores, big_negative)
    new_scores = jnp.where(seen, new_scores, big_negative)
    peak = jnp.maximum(jnp.max(scores, axis=1), jnp.max(new_scores, axis=1))
    peak = peak.astype(bf16)
    level = peak.astype(f32)[:, None]
    weights = jnp.where(usable, jnp.exp(scores - level), 0.0)
    new_weights = jnp.where(seen, jnp.exp(new_scores - level), 0.0)
    total = jnp.sum(weights, axis=1) + jnp.sum(new_weights, axis=1)
    accum = jnp.dot(weights.astype(bf16), cache[:, head:], preferred_element_type=f32)
    rounded = new_weights.astype(bf16).astype(f32)
    values = fresh[:, head:].astype(f32)
    accum = accum + rounded[:, :1] * values[:1] + rounded[:, 1:] * values[1:]
    mixed = (accum / total[:, None]).astype(bf16)
    high = total.astype(bf16)
    low = (total - high.astype(f32)).astype(bf16)
    stats = jnp.concatenate([part.reshape(2, group) for part in (peak, high, low)], axis=1)
    stats = jnp.pad(stats, ((0, 0), (0, 128 - 3 * group)))
    return jnp.concatenate([mixed.reshape(2, group * head), stats], axis=1)


def merge_sides(parts, group):
    rows = parts.shape[1]
    width = parts.shape[2] - 128
    stats = parts[:, :, width:].astype(f32)
    peak = stats[:, :, :group]
    total = stats[:, :, group : 2 * group] + stats[:, :, 2 * group : 3 * group]
    weight = total * jnp.exp(peak - jnp.max(peak, axis=0, keepdims=True))
    weight = weight / jnp.sum(weight, axis=0, keepdims=True)
    mixed = parts[:, :, :width].astype(f32).reshape(2, rows, group, width // group)
    return jnp.sum(mixed * weight[..., None], axis=0).reshape(rows, width).astype(bf16)


def local(hidden_in, queries, kv_cache, new_kv, lengths, out_weight, norm_gain, gate_weight, up_weight, down_weight):
    side_index = lax.axis_index("side")
    group = queries.shape[2]
    rows = hidden_in.shape[0] * 2
    cols = hidden_in.shape[2]
    hidden = gate_weight.shape[1]
    part = hidden // YS

    own = partial_attention(queries, kv_cache, new_kv, lengths, side_index, side_index == SIDES - 1)
    everyone = spread(own, ROWS, YS * ZS)
    attended = merge_sides(everyone.reshape(SIDES, rows, own.shape[1]), group)
    attn_part = jnp.dot(attended, out_weight, preferred_element_type=f32)
    attn_sum = jnp.sum(spread(attn_part.astype(bf16), GY, 8).astype(f32), axis=0)
    middle = hidden_in.reshape(rows, cols).astype(f32) + attn_sum

    squares = jnp.sum(middle * middle, axis=1, keepdims=True)
    scaled = (middle * norm_gain).astype(bf16)
    gate_term = jnp.dot(scaled, gate_weight, preferred_element_type=f32).astype(bf16)
    up_term = jnp.dot(scaled, up_weight, preferred_element_type=f32).astype(bf16)
    high = squares.astype(bf16)
    low = (squares - high.astype(f32)).astype(bf16)
    pair = jnp.pad(jnp.concatenate([high, low], axis=1), ((0, 0), (0, 126)))
    blocks = [
        jnp.concatenate([gate_term[:, j * part : (j + 1) * part], up_term[:, j * part : (j + 1) * part], pair], axis=1)
        for j in range(YS)
    ]
    over_y = lax.all_to_all(jnp.stack(blocks), Y, 0, 0).astype(f32)
    over_y = jnp.sum(over_y, axis=0)
    squares = over_y[:, 2 * part : 2 * part + 1] + over_y[:, 2 * part + 1 : 2 * part + 2]
    high = squares.astype(bf16)
    low = (squares - high.astype(f32)).astype(bf16)
    pair = jnp.pad(jnp.concatenate([high, low], axis=1), ((0, 0), (0, 126)))
    to_z = jnp.concatenate([over_y[:, : 2 * part].astype(bf16), pair], axis=1)
    over_z = lax.all_to_all(to_z.reshape(ZS, rows // ZS, -1), "z", 0, 0).astype(f32)
    over_z = jnp.sum(over_z, axis=0)
    squares = over_z[:, 2 * part : 2 * part + 1] + over_z[:, 2 * part + 1 : 2 * part + 2]
    factor = lax.rsqrt(squares / D + 1e-05)
    gate = over_z[:, :part] * factor
    up = over_z[:, part : 2 * part] * factor
    activated = (jax.nn.silu(gate) * up).astype(bf16)
    along_z = spread(activated, "z", ZS).reshape(rows, part)
    along_y = spread(along_z, Y, YS)
    ffn_part = sum(
        jnp.dot(along_y[j], down_weight[j * part : (j + 1) * part], preferred_element_type=f32) for j in range(YS)
    )
    ffn_sum = jnp.sum(spread(ffn_part.astype(bf16), GY, 8).astype(f32), axis=0)
    return (middle + ffn_sum).astype(bf16).reshape(hidden_in.shape)


def solution(mesh):
    fine = Mesh(mesh.devices.reshape(2, 2, 16, 4, 2), ("side", "yhi", "z", "x", "core"))
    in_specs = (
        P(None, None, ROWS),
        P(("yhi", "z"), None, GY, None),
        P(("yhi", "z"), "side", GY, None),
        P(("yhi", "z"), None, GY, None),
        P(("yhi", "z")),
        P(GY, ROWS),
        P(ROWS),
        P(ROWS, GY),
        P(ROWS, GY),
        P(GY, ROWS),
    )
    return jax.shard_map(local, mesh=fine, in_specs=in_specs, out_specs=P(None, None, ROWS), check_vma=False)
```

```python
import functools
import math

import jax
import jax.numpy as jnp
from jax import lax
from jax.experimental import pallas as pl
from jax.experimental.pallas import tpu as pltpu
from jax.sharding import Mesh, PartitionSpec as P

D = 8192
EPS = 1e-05
big_negative = -1e30
bf16 = jnp.bfloat16
f32 = jnp.float32

LANES = 128
SIDES, YS, ZQ, ZP = 2, 4, 8, 2
ZS = ZQ * ZP
ROWS = ("side", "yhi", "zq", "zp")
Y = ("side", "yhi")
Z = ("zq", "zp")
NEAR = ("side", "yhi", "zp")
GY = ("x", "core")
GYS = 8


def spread(value, axes, count):
    return lax.all_to_all(jnp.broadcast_to(value, (count, *value.shape)), axes, 0, 0)


SMALL = pltpu.CompilerParams(vmem_limit_bytes=12 * 2**20)


def vmem(count):
    return [pl.BlockSpec(memory_space=pltpu.VMEM)] * count


def split(total):
    high = total.astype(bf16).astype(f32)
    return high, total - high


def attention_kernel(length_ref, query_ref, cache_ref, fresh_ref, out_ref):
    side = lax.axis_index("side")
    half, doubled = cache_ref.shape
    head = doubled // 2
    pairs = query_ref.shape[0]
    group = pairs // 2
    scale = 1.0 / math.sqrt(head)
    contract_last = (((1,), (1,)), ((), ()))
    query = query_ref[...]
    scores = lax.dot_general(query, cache_ref[:, :head], contract_last, preferred_element_type=f32) * scale
    usable = side * half + lax.broadcasted_iota(jnp.int32, (pairs, half), 1) < length_ref[0]
    scores = jnp.where(usable, scores, big_negative)
    fresh = fresh_ref[...].astype(f32)
    draft = lax.broadcasted_iota(jnp.int32, (pairs, 1), 0) // group
    wide = query.astype(f32)
    new_scores, seen = [], []
    for u in range(2):
        seen.append((draft >= u) & (side == SIDES - 1))
        score = jnp.sum(wide * fresh[u : u + 1, :head], axis=1, keepdims=True) * scale
        new_scores.append(jnp.where(seen[u], score, big_negative))
    peak = jnp.max(scores, axis=1, keepdims=True)
    peak = jnp.maximum(peak, jnp.maximum(new_scores[0], new_scores[1]))
    peak = peak.astype(bf16).astype(f32)
    weights = jnp.where(usable, jnp.exp(scores - peak), 0.0)
    total = jnp.sum(weights, axis=1, keepdims=True)
    accum = jnp.dot(weights.astype(bf16), cache_ref[:, head:], preferred_element_type=f32)
    for u in range(2):
        weight = jnp.where(seen[u], jnp.exp(new_scores[u] - peak), 0.0)
        total = total + weight
        accum = accum + weight.astype(bf16).astype(f32) * fresh[u : u + 1, head:]
    mixed = accum / total
    high, low = split(total)
    lane = lax.broadcasted_iota(jnp.int32, (pairs, LANES), 1)
    row = lax.broadcasted_iota(jnp.int32, (pairs, LANES), 0) % group
    stats = jnp.where(lane == row, peak, 0.0)
    stats = jnp.where(lane == row + group, high, stats)
    stats = jnp.where(lane == row + 2 * group, low, stats)
    stats = [jnp.sum(stats[t * group : (t + 1) * group], axis=0, keepdims=True) for t in range(2)]
    for i in range(group):
        both = jnp.concatenate([mixed[i : i + 1], mixed[group + i : group + i + 1]], axis=0)
        out_ref[:, i * head : (i + 1) * head] = both.astype(bf16)
    out_ref[:, group * head :] = jnp.concatenate(stats, axis=0).astype(bf16)


def project_kernel(group, parts_ref, weight_ref, out_ref):
    width = weight_ref.shape[0]
    head = width // group
    stats = [parts_ref[s, :, width:].astype(f32) for s in range(SIDES)]
    totals = [stat[:, group : 2 * group] + stat[:, 2 * group : 3 * group] for stat in stats]
    peaks = [stat[:, :group] for stat in stats]
    peak = jnp.maximum(peaks[0], peaks[1])
    shares = [totals[s] * jnp.exp(peaks[s] - peak) for s in range(SIDES)]
    whole = shares[0] + shares[1]
    shares = [share / whole for share in shares]
    merged = []
    for i in range(group):
        columns = slice(i * head, (i + 1) * head)
        value = parts_ref[0, :, columns].astype(f32) * shares[0][:, i : i + 1]
        value = value + parts_ref[1, :, columns].astype(f32) * shares[1][:, i : i + 1]
        merged.append(value.astype(bf16))
    total = jnp.dot(jnp.concatenate(merged, axis=1), weight_ref[...], preferred_element_type=f32).astype(bf16)
    for k in range(out_ref.shape[0]):
        out_ref[k] = total


def gate_kernel(parts_ref, hidden_ref, gain_ref, gate_ref, up_ref, middle_ref, out_ref):
    middle = hidden_ref[...].astype(f32)
    for k in range(parts_ref.shape[0]):
        middle = middle + parts_ref[k].astype(f32)
    middle_ref[...] = middle
    rows = middle.shape[0]
    step = rows // ZS
    high, low = split(jnp.sum(middle * middle, axis=1, keepdims=True))
    lane = lax.broadcasted_iota(jnp.int32, (rows, LANES), 1)
    stats = jnp.where(lane == 0, high, jnp.where(lane == 1, low, 0.0))
    scaled = middle * gain_ref[...]

    def regroup(value):
        pieces = [value[(q * ZP + p) * step : (q * ZP + p + 1) * step] for p in range(ZP) for q in range(ZQ)]
        return jnp.concatenate(pieces, axis=0).astype(bf16)

    scaled, stats = regroup(scaled), regroup(stats)
    part = gate_ref.shape[1] // YS
    half = rows // ZP
    for y in range(YS):
        columns = slice(y * part, (y + 1) * part)
        for start, ref in ((0, gate_ref), (part, up_ref)):
            term = jnp.dot(scaled, ref[:, columns], preferred_element_type=f32).astype(bf16)
            for p in range(ZP):
                out_ref[y * ZP + p, :, start : start + part] = term[p * half : (p + 1) * half]
        for p in range(ZP):
            out_ref[y * ZP + p, :, 2 * part :] = stats[p * half : (p + 1) * half]


def sum_kernel(parts_ref, out_ref):
    total = parts_ref[0].astype(f32)
    for k in range(1, parts_ref.shape[0]):
        total = total + parts_ref[k].astype(f32)
    width = total.shape[1] - LANES
    stats = total[:, width:]
    high, low = split(stats[:, :1] + stats[:, 1:2])
    lane = lax.broadcasted_iota(jnp.int32, stats.shape, 1)
    stats = jnp.where(lane == 0, high, jnp.where(lane == 1, low, 0.0)).astype(bf16)
    total = total[:, :width].astype(bf16)
    step = out_ref.shape[1]
    for q in range(out_ref.shape[0]):
        out_ref[q, :, :width] = total[q * step : (q + 1) * step]
        out_ref[q, :, width:] = stats[q * step : (q + 1) * step]


def activate_kernel(parts_ref, out_ref):
    total = parts_ref[0].astype(f32)
    for k in range(1, parts_ref.shape[0]):
        total = total + parts_ref[k].astype(f32)
    part = out_ref.shape[2]
    squares = total[:, 2 * part : 2 * part + 1] + total[:, 2 * part + 1 : 2 * part + 2]
    factor = lax.rsqrt(squares / D + EPS)
    gate = total[:, :part] * factor
    up = total[:, part : 2 * part] * factor
    activated = (gate / (1.0 + jnp.exp(-gate)) * up).astype(bf16)
    for k in range(out_ref.shape[0]):
        out_ref[k] = activated


def down_kernel(active_ref, weight_ref, out_ref):
    part = active_ref.shape[2]
    total = jnp.dot(active_ref[0], weight_ref[:part], preferred_element_type=f32)
    for y in range(1, YS):
        total = total + jnp.dot(active_ref[y], weight_ref[y * part : (y + 1) * part], preferred_element_type=f32)
    total = total.astype(bf16)
    for k in range(out_ref.shape[0]):
        out_ref[k] = total


def local(hidden_in, queries, kv_cache, new_kv, lengths, out_weight, norm_gain, gate_weight, up_weight, down_weight):
    group, head = queries.shape[2:]
    rows = hidden_in.shape[0] * 2
    cols = hidden_in.shape[2]
    width = out_weight.shape[0]
    part = gate_weight.shape[1] // YS
    step = rows // ZS
    shape = jax.ShapeDtypeStruct
    hidden = hidden_in.reshape(rows, cols)

    own = pl.pallas_call(
        attention_kernel,
        out_shape=shape((2, width + LANES), bf16),
        in_specs=[pl.BlockSpec(memory_space=pltpu.SMEM)] + vmem(3),
        out_specs=vmem(1)[0],
        name="attention",
        compiler_params=SMALL,
    )(lengths, queries.reshape(2 * group, head), kv_cache.reshape(-1, 2 * head), new_kv.reshape(2, 2 * head))
    everyone = spread(own, ROWS, YS * ZS).reshape(SIDES, rows, width + LANES)
    head_parts = pl.pallas_call(
        functools.partial(project_kernel, group),
        out_shape=shape((GYS, rows, cols), bf16),
        in_specs=vmem(2),
        out_specs=vmem(1)[0],
        name="project",
        compiler_params=SMALL,
    )(everyone, out_weight)
    head_parts = lax.all_to_all(head_parts, GY, 0, 0)
    middle, terms = pl.pallas_call(
        gate_kernel,
        out_shape=[shape((rows, cols), f32), shape((YS * ZP, rows // ZP, 2 * part + LANES), bf16)],
        in_specs=vmem(5),
        out_specs=vmem(2),
        name="gate_up",
        compiler_params=SMALL,
    )(head_parts, hidden, norm_gain.reshape(1, cols), gate_weight, up_weight)
    terms = lax.all_to_all(terms, NEAR, 0, 0)
    terms = pl.pallas_call(
        sum_kernel,
        out_shape=shape((ZQ, step, 2 * part + LANES), bf16),
        in_specs=vmem(1),
        out_specs=vmem(1)[0],
        name="near_sum",
        compiler_params=SMALL,
    )(terms)
    terms = lax.all_to_all(terms, "zq", 0, 0)
    activated = pl.pallas_call(
        activate_kernel,
        out_shape=shape((ZS, step, part), bf16),
        in_specs=vmem(1),
        out_specs=vmem(1)[0],
        name="activate",
        compiler_params=SMALL,
    )(terms)
    along_z = lax.all_to_all(activated, Z, 0, 0).reshape(rows, part)
    along_y = spread(along_z, Y, YS)
    ffn_parts = pl.pallas_call(
        down_kernel,
        out_shape=shape((GYS, rows, cols), bf16),
        in_specs=vmem(2),
        out_specs=vmem(1)[0],
        name="down",
        compiler_params=SMALL,
    )(along_y, down_weight)
    ffn_sum = jnp.sum(lax.all_to_all(ffn_parts, GY, 0, 0).astype(f32), axis=0)
    return (middle + ffn_sum).astype(bf16).reshape(hidden_in.shape)


def solution(mesh):
    fine = Mesh(mesh.devices.reshape(2, 2, ZQ, ZP, 4, 2), ("side", "yhi", "zq", "zp", "x", "core"))
    requests = ("yhi", "zq", "zp")
    in_specs = (
        P(None, None, ROWS),
        P(requests, None, GY, None),
        P(requests, "side", GY, None),
        P(requests, None, GY, None),
        P(requests),
        P(GY, ROWS),
        P(ROWS),
        P(ROWS, GY),
        P(ROWS, GY),
        P(GY, ROWS),
    )
    return jax.shard_map(local, mesh=fine, in_specs=in_specs, out_specs=P(None, None, ROWS), check_vma=False)
```

```python
import functools
import math

import jax
import jax.numpy as jnp
from jax import lax
from jax.experimental import pallas as pl
from jax.experimental.pallas import tpu as pltpu
from jax.sharding import Mesh, PartitionSpec as P

D = 8192
EPS = 1e-05
big_negative = -1e30
bf16 = jnp.bfloat16
f32 = jnp.float32

LANES = 128
SIDES, YS, ZQ, ZP = 2, 4, 8, 2
ZS = ZQ * ZP
ROWS = ("side", "yhi", "zq", "zp")
Y = ("side", "yhi")
Z = ("zq", "zp")
NEAR = ("side", "yhi", "zp")
GY = ("x", "core")
GYS = 8


def spread(value, axes, count):
    return lax.all_to_all(jnp.broadcast_to(value, (count, *value.shape)), axes, 0, 0)


SMALL = pltpu.CompilerParams(vmem_limit_bytes=12 * 2**20)


def vmem(count):
    return [pl.BlockSpec(memory_space=pltpu.VMEM)] * count


def split(total):
    high = total.astype(bf16).astype(f32)
    return high, total - high


def attention_kernel(
    length_ref,
    query_hbm,
    cache_hbm,
    fresh_hbm,
    hidden_hbm,
    gain_hbm,
    out_ref,
    hidden_ref,
    gain_ref,
    query_ref,
    cache_ref,
    fresh_ref,
    arrived,
):
    moves = (
        (cache_hbm, cache_ref),
        (query_hbm, query_ref),
        (fresh_hbm, fresh_ref),
        (hidden_hbm, hidden_ref),
        (gain_hbm, gain_ref),
    )
    copies = [pltpu.make_async_copy(source, target, arrived.at[k]) for k, (source, target) in enumerate(moves)]
    for copy in copies:
        copy.start()
    for copy in copies:
        copy.wait()
    side = lax.axis_index("side")
    half, doubled = cache_ref.shape
    head = doubled // 2
    pairs = query_ref.shape[0]
    group = pairs // 2
    scale = 1.0 / math.sqrt(head)
    contract_last = (((1,), (1,)), ((), ()))
    query = query_ref[...]
    scores = lax.dot_general(query, cache_ref[:, :head], contract_last, preferred_element_type=f32) * scale
    usable = side * half + lax.broadcasted_iota(jnp.int32, (pairs, half), 1) < length_ref[0]
    scores = jnp.where(usable, scores, big_negative)
    fresh = fresh_ref[...].astype(f32)
    draft = lax.broadcasted_iota(jnp.int32, (pairs, 1), 0) // group
    wide = query.astype(f32)
    new_scores, seen = [], []
    for u in range(2):
        seen.append((draft >= u) & (side == SIDES - 1))
        score = jnp.sum(wide * fresh[u : u + 1, :head], axis=1, keepdims=True) * scale
        new_scores.append(jnp.where(seen[u], score, big_negative))
    peak = jnp.max(scores, axis=1, keepdims=True)
    peak = jnp.maximum(peak, jnp.maximum(new_scores[0], new_scores[1]))
    peak = peak.astype(bf16).astype(f32)
    weights = jnp.where(usable, jnp.exp(scores - peak), 0.0)
    total = jnp.sum(weights, axis=1, keepdims=True)
    accum = jnp.dot(weights.astype(bf16), cache_ref[:, head:], preferred_element_type=f32)
    for u in range(2):
        weight = jnp.where(seen[u], jnp.exp(new_scores[u] - peak), 0.0)
        total = total + weight
        accum = accum + weight.astype(bf16).astype(f32) * fresh[u : u + 1, head:]
    mixed = accum / total
    high, low = split(total)
    lane = lax.broadcasted_iota(jnp.int32, (pairs, LANES), 1)
    row = lax.broadcasted_iota(jnp.int32, (pairs, LANES), 0) % group
    stats = jnp.where(lane == row, peak, 0.0)
    stats = jnp.where(lane == row + group, high, stats)
    stats = jnp.where(lane == row + 2 * group, low, stats)
    stats = [jnp.sum(stats[t * group : (t + 1) * group], axis=0, keepdims=True) for t in range(2)]
    for i in range(group):
        both = jnp.concatenate([mixed[i : i + 1], mixed[group + i : group + i + 1]], axis=0)
        out_ref[:, i * head : (i + 1) * head] = both.astype(bf16)
    out_ref[:, group * head :] = jnp.concatenate(stats, axis=0).astype(bf16)


def project_kernel(group, parts_ref, weight_ref, out_ref):
    width = weight_ref.shape[0]
    head = width // group
    stats = [parts_ref[s, :, width:].astype(f32) for s in range(SIDES)]
    totals = [stat[:, group : 2 * group] + stat[:, 2 * group : 3 * group] for stat in stats]
    peaks = [stat[:, :group] for stat in stats]
    peak = jnp.maximum(peaks[0], peaks[1])
    shares = [totals[s] * jnp.exp(peaks[s] - peak) for s in range(SIDES)]
    whole = shares[0] + shares[1]
    shares = [share / whole for share in shares]
    merged = []
    for i in range(group):
        columns = slice(i * head, (i + 1) * head)
        value = parts_ref[0, :, columns].astype(f32) * shares[0][:, i : i + 1]
        value = value + parts_ref[1, :, columns].astype(f32) * shares[1][:, i : i + 1]
        merged.append(value.astype(bf16))
    total = jnp.dot(jnp.concatenate(merged, axis=1), weight_ref[...], preferred_element_type=f32).astype(bf16)
    for k in range(out_ref.shape[0]):
        out_ref[k] = total


def gate_kernel(parts_ref, hidden_ref, gain_ref, gate_ref, up_ref, middle_ref, out_ref):
    middle = hidden_ref[...].astype(f32)
    for k in range(parts_ref.shape[0]):
        middle = middle + parts_ref[k].astype(f32)
    middle_ref[...] = middle
    rows = middle.shape[0]
    step = rows // ZS
    high, low = split(jnp.sum(middle * middle, axis=1, keepdims=True))
    lane = lax.broadcasted_iota(jnp.int32, (rows, LANES), 1)
    stats = jnp.where(lane == 0, high, jnp.where(lane == 1, low, 0.0))
    scaled = middle * gain_ref[...]

    def regroup(value):
        pieces = [value[(q * ZP + p) * step : (q * ZP + p + 1) * step] for p in range(ZP) for q in range(ZQ)]
        return jnp.concatenate(pieces, axis=0).astype(bf16)

    scaled, stats = regroup(scaled), regroup(stats)
    part = gate_ref.shape[1] // YS
    half = rows // ZP
    for y in range(YS):
        columns = slice(y * part, (y + 1) * part)
        for start, ref in ((0, gate_ref), (part, up_ref)):
            term = jnp.dot(scaled, ref[:, columns], preferred_element_type=f32).astype(bf16)
            for p in range(ZP):
                out_ref[y * ZP + p, :, start : start + part] = term[p * half : (p + 1) * half]
        for p in range(ZP):
            out_ref[y * ZP + p, :, 2 * part :] = stats[p * half : (p + 1) * half]


def sum_kernel(parts_ref, out_ref):
    total = parts_ref[0].astype(f32)
    for k in range(1, parts_ref.shape[0]):
        total = total + parts_ref[k].astype(f32)
    width = total.shape[1] - LANES
    stats = total[:, width:]
    high, low = split(stats[:, :1] + stats[:, 1:2])
    lane = lax.broadcasted_iota(jnp.int32, stats.shape, 1)
    stats = jnp.where(lane == 0, high, jnp.where(lane == 1, low, 0.0)).astype(bf16)
    total = total[:, :width].astype(bf16)
    step = out_ref.shape[1]
    for q in range(out_ref.shape[0]):
        out_ref[q, :, :width] = total[q * step : (q + 1) * step]
        out_ref[q, :, width:] = stats[q * step : (q + 1) * step]


def activate_kernel(parts_ref, out_ref):
    total = parts_ref[0].astype(f32)
    for k in range(1, parts_ref.shape[0]):
        total = total + parts_ref[k].astype(f32)
    part = out_ref.shape[2]
    squares = total[:, 2 * part : 2 * part + 1] + total[:, 2 * part + 1 : 2 * part + 2]
    factor = lax.rsqrt(squares / D + EPS)
    gate = total[:, :part] * factor
    up = total[:, part : 2 * part] * factor
    activated = (gate / (1.0 + jnp.exp(-gate)) * up).astype(bf16)
    for k in range(out_ref.shape[0]):
        out_ref[k] = activated


def down_kernel(active_ref, weight_ref, out_ref):
    part = active_ref.shape[2]
    total = jnp.dot(active_ref[0], weight_ref[:part], preferred_element_type=f32)
    for y in range(1, YS):
        total = total + jnp.dot(active_ref[y], weight_ref[y * part : (y + 1) * part], preferred_element_type=f32)
    total = total.astype(bf16)
    for k in range(out_ref.shape[0]):
        out_ref[k] = total


def local(hidden_in, queries, kv_cache, new_kv, lengths, out_weight, norm_gain, gate_weight, up_weight, down_weight):
    group, head = queries.shape[2:]
    rows = hidden_in.shape[0] * 2
    cols = hidden_in.shape[2]
    width = out_weight.shape[0]
    part = gate_weight.shape[1] // YS
    step = rows // ZS
    shape = jax.ShapeDtypeStruct

    own, hidden, gain = pl.pallas_call(
        attention_kernel,
        out_shape=[shape((2, width + LANES), bf16), shape((rows, cols), bf16), shape((1, cols), f32)],
        in_specs=[pl.BlockSpec(memory_space=pltpu.SMEM)] + [pl.BlockSpec(memory_space=pltpu.HBM)] * 5,
        out_specs=vmem(3),
        scratch_shapes=[
            pltpu.VMEM((2 * group, head), bf16),
            pltpu.VMEM((kv_cache.shape[1], 2 * head), bf16),
            pltpu.VMEM((2, 2 * head), bf16),
            pltpu.SemaphoreType.DMA((5,)),
        ],
        name="attention",
        compiler_params=SMALL,
    )(
        lengths,
        *(
            pltpu.with_memory_space_constraint(value, pltpu.HBM)
            for value in (
                queries.reshape(2 * group, head),
                kv_cache.reshape(-1, 2 * head),
                new_kv.reshape(2, 2 * head),
                hidden_in.reshape(rows, cols),
                norm_gain.reshape(1, cols),
            )
        ),
    )
    along_z = spread(own, Z, ZS).reshape(2 * ZS, width + LANES)
    everyone = spread(along_z, Y, YS).reshape(SIDES, rows, width + LANES)
    head_parts = pl.pallas_call(
        functools.partial(project_kernel, group),
        out_shape=shape((GYS, rows, cols), bf16),
        in_specs=vmem(2),
        out_specs=vmem(1)[0],
        name="project",
        compiler_params=SMALL,
    )(everyone, out_weight)
    head_parts = lax.all_to_all(head_parts, GY, 0, 0)
    middle, terms = pl.pallas_call(
        gate_kernel,
        out_shape=[shape((rows, cols), f32), shape((YS * ZP, rows // ZP, 2 * part + LANES), bf16)],
        in_specs=vmem(5),
        out_specs=vmem(2),
        name="gate_up",
        compiler_params=SMALL,
    )(head_parts, hidden, gain, gate_weight, up_weight)
    terms = lax.all_to_all(terms, NEAR, 0, 0)
    terms = pl.pallas_call(
        sum_kernel,
        out_shape=shape((ZQ, step, 2 * part + LANES), bf16),
        in_specs=vmem(1),
        out_specs=vmem(1)[0],
        name="near_sum",
        compiler_params=SMALL,
    )(terms)
    terms = lax.all_to_all(terms, "zq", 0, 0)
    activated = pl.pallas_call(
        activate_kernel,
        out_shape=shape((ZS, step, part), bf16),
        in_specs=vmem(1),
        out_specs=vmem(1)[0],
        name="activate",
        compiler_params=SMALL,
    )(terms)
    along_z = lax.all_to_all(activated, Z, 0, 0).reshape(rows, part)
    along_y = spread(along_z, Y, YS)
    ffn_parts = pl.pallas_call(
        down_kernel,
        out_shape=shape((GYS, rows, cols), bf16),
        in_specs=vmem(2),
        out_specs=vmem(1)[0],
        name="down",
        compiler_params=SMALL,
    )(along_y, down_weight)
    ffn_sum = jnp.sum(lax.all_to_all(ffn_parts, GY, 0, 0).astype(f32), axis=0)
    return (middle + ffn_sum).astype(bf16).reshape(hidden_in.shape)


def solution(mesh):
    fine = Mesh(mesh.devices.reshape(2, 2, ZQ, ZP, 4, 2), ("side", "yhi", "zq", "zp", "x", "core"))
    requests = ("yhi", "zq", "zp")
    in_specs = (
        P(None, None, ROWS),
        P(requests, None, GY, None),
        P(requests, "side", GY, None),
        P(requests, None, GY, None),
        P(requests),
        P(GY, ROWS),
        P(ROWS),
        P(ROWS, GY),
        P(ROWS, GY),
        P(GY, ROWS),
    )
    return jax.shard_map(local, mesh=fine, in_specs=in_specs, out_specs=P(None, None, ROWS), check_vma=False)
```

```python
import functools
import math

import jax
import jax.numpy as jnp
from jax import lax
from jax.experimental import pallas as pl
from jax.experimental.pallas import tpu as pltpu
from jax.sharding import Mesh, PartitionSpec as P

D = 8192
EPS = 1e-05
big_negative = -1e30
bf16 = jnp.bfloat16
f32 = jnp.float32

LANES, TALL = 128, 8
SIDES, YS, ZQ, ZP = 2, 4, 8, 2
ZS = ZQ * ZP
ROWS = ("side", "yhi", "zq", "zp")
Y = ("side", "yhi")
Z = ("zq", "zp")
NEAR = ("side", "yhi", "zp")
GY = ("x", "core")
GYS = 8


def spread(value, axes, count):
    return lax.all_to_all(jnp.broadcast_to(value, (count, *value.shape)), axes, 0, 0)


SMALL = pltpu.CompilerParams(vmem_limit_bytes=12 * 2**20)


def vmem(count):
    return [pl.BlockSpec(memory_space=pltpu.VMEM)] * count


def split(total):
    high = total.astype(bf16).astype(f32)
    return high, total - high


def attention_kernel(
    length_ref,
    query_hbm,
    cache_hbm,
    fresh_hbm,
    hidden_hbm,
    gain_hbm,
    out_ref,
    hidden_ref,
    gain_ref,
    query_ref,
    cache_ref,
    fresh_ref,
    arrived,
):
    moves = (
        (cache_hbm, cache_ref),
        (query_hbm, query_ref),
        (fresh_hbm, fresh_ref),
        (hidden_hbm, hidden_ref),
        (gain_hbm, gain_ref),
    )
    copies = [pltpu.make_async_copy(source, target, arrived.at[k]) for k, (source, target) in enumerate(moves)]
    for copy in copies:
        copy.start()
    for copy in copies:
        copy.wait()
    side = lax.axis_index("side")
    half, doubled = cache_ref.shape
    head = doubled // 2
    pairs = query_ref.shape[0]
    group = pairs // 2
    scale = 1.0 / math.sqrt(head)
    contract_last = (((1,), (1,)), ((), ()))
    query = query_ref[...]
    scores = lax.dot_general(query, cache_ref[:, :head], contract_last, preferred_element_type=f32) * scale
    usable = side * half + lax.broadcasted_iota(jnp.int32, (pairs, half), 1) < length_ref[0]
    scores = jnp.where(usable, scores, big_negative)
    fresh = fresh_ref[...].astype(f32)
    draft = lax.broadcasted_iota(jnp.int32, (pairs, 1), 0) // group
    wide = query.astype(f32)
    new_scores, seen = [], []
    for u in range(2):
        seen.append((draft >= u) & (side == SIDES - 1))
        score = jnp.sum(wide * fresh[u : u + 1, :head], axis=1, keepdims=True) * scale
        new_scores.append(jnp.where(seen[u], score, big_negative))
    peak = jnp.max(scores, axis=1, keepdims=True)
    peak = jnp.maximum(peak, jnp.maximum(new_scores[0], new_scores[1]))
    peak = peak.astype(bf16).astype(f32)
    weights = jnp.where(usable, jnp.exp(scores - peak), 0.0)
    total = jnp.sum(weights, axis=1, keepdims=True)
    accum = jnp.dot(weights.astype(bf16), cache_ref[:, head:], preferred_element_type=f32)
    for u in range(2):
        weight = jnp.where(seen[u], jnp.exp(new_scores[u] - peak), 0.0)
        total = total + weight
        accum = accum + weight.astype(bf16).astype(f32) * fresh[u : u + 1, head:]
    mixed = accum / total
    high, low = split(total)
    lane = lax.broadcasted_iota(jnp.int32, (pairs, LANES), 1)
    row = lax.broadcasted_iota(jnp.int32, (pairs, LANES), 0) % group
    stats = jnp.where(lane == row, peak, 0.0)
    stats = jnp.where(lane == row + group, high, stats)
    stats = jnp.where(lane == row + 2 * group, low, stats)
    stats = [jnp.sum(stats[t * group : (t + 1) * group], axis=0, keepdims=True) for t in range(2)]
    for i in range(group):
        both = jnp.concatenate([mixed[i : i + 1], mixed[group + i : group + i + 1]], axis=0)
        out_ref[:, i * head : (i + 1) * head] = both.astype(bf16)
    out_ref[:, group * head :] = jnp.concatenate(stats, axis=0).astype(bf16)


def project_kernel(group, parts_ref, weight_ref, out_ref):
    width = weight_ref.shape[0]
    head = width // group
    stats = [parts_ref[s, :, width:].astype(f32) for s in range(SIDES)]
    totals = [stat[:, group : 2 * group] + stat[:, 2 * group : 3 * group] for stat in stats]
    peaks = [stat[:, :group] for stat in stats]
    peak = jnp.maximum(peaks[0], peaks[1])
    shares = [totals[s] * jnp.exp(peaks[s] - peak) for s in range(SIDES)]
    whole = shares[0] + shares[1]
    shares = [share / whole for share in shares]
    merged = []
    for i in range(group):
        columns = slice(i * head, (i + 1) * head)
        value = parts_ref[0, :, columns].astype(f32) * shares[0][:, i : i + 1]
        value = value + parts_ref[1, :, columns].astype(f32) * shares[1][:, i : i + 1]
        merged.append(value.astype(bf16))
    total = jnp.dot(jnp.concatenate(merged, axis=1), weight_ref[...], preferred_element_type=f32).astype(bf16)
    for k in range(out_ref.shape[0]):
        out_ref[k] = total


def gate_kernel(parts_ref, hidden_ref, gain_ref, gate_ref, up_ref, middle_ref, out_ref):
    middle = hidden_ref[...].astype(f32)
    for k in range(parts_ref.shape[0]):
        middle = middle + parts_ref[k].astype(f32)
    middle_ref[...] = middle
    rows = middle.shape[0]
    step = rows // ZS
    high, low = split(jnp.sum(middle * middle, axis=1, keepdims=True))
    scaled = middle * gain_ref[...]

    def regroup(value):
        pieces = [value[(q * ZP + p) * step : (q * ZP + p + 1) * step] for p in range(ZP) for q in range(ZQ)]
        return jnp.concatenate(pieces, axis=0)

    scaled, high, low = regroup(scaled).astype(bf16), regroup(high), regroup(low)
    part = gate_ref.shape[1] // YS
    tall = out_ref.shape[1]
    count = rows // ZP // tall
    lane = lax.broadcasted_iota(jnp.int32, (tall, LANES), 1)
    for p in range(ZP):
        stats = jnp.zeros((tall, LANES), f32)
        for g in range(count):
            block = slice((p * count + g) * tall, (p * count + g + 1) * tall)
            stats = jnp.where(lane == 2 * g, high[block], jnp.where(lane == 2 * g + 1, low[block], stats))
        for y in range(YS):
            out_ref[y * ZP + p, :, 2 * part * count :] = stats.astype(bf16)
    for y in range(YS):
        columns = slice(y * part, (y + 1) * part)
        for start, ref in ((0, gate_ref), (part, up_ref)):
            term = jnp.dot(scaled, ref[:, columns], preferred_element_type=f32)
            for p in range(ZP):
                for g in range(count):
                    block = term[(p * count + g) * tall : (p * count + g + 1) * tall].astype(bf16)
                    out_ref[y * ZP + p, :, 2 * part * g + start : 2 * part * g + start + part] = block


def sum_kernel(parts_ref, out_ref):
    total = parts_ref[0].astype(f32)
    for k in range(1, parts_ref.shape[0]):
        total = total + parts_ref[k].astype(f32)
    step = out_ref.shape[1]
    width = out_ref.shape[2] - LANES
    tall = total.shape[0]
    each = tall // step
    count = out_ref.shape[0] // each
    lane = lax.broadcasted_iota(jnp.int32, (tall, LANES), 1)
    pairs = total[:, width * count :]
    for g in range(count):
        high, low = split(pairs[:, 2 * g : 2 * g + 1] + pairs[:, 2 * g + 1 : 2 * g + 2])
        stats = jnp.where(lane == 0, high, jnp.where(lane == 1, low, 0.0))
        for e in range(each):
            rows = slice(e * step, (e + 1) * step)
            out_ref[g * each + e, :, :width] = total[rows, g * width : (g + 1) * width].astype(bf16)
            out_ref[g * each + e, :, width:] = stats[rows].astype(bf16)


def activate_kernel(parts_ref, out_ref):
    total = parts_ref[0].astype(f32)
    for k in range(1, parts_ref.shape[0]):
        total = total + parts_ref[k].astype(f32)
    part = out_ref.shape[2]
    squares = total[:, 2 * part : 2 * part + 1] + total[:, 2 * part + 1 : 2 * part + 2]
    factor = lax.rsqrt(squares / D + EPS)
    gate = total[:, :part] * factor
    up = total[:, part : 2 * part] * factor
    activated = (gate / (1.0 + jnp.exp(-gate)) * up).astype(bf16)
    for k in range(out_ref.shape[0]):
        out_ref[k] = activated


def down_kernel(active_ref, weight_ref, out_ref):
    part = active_ref.shape[2]
    total = jnp.dot(active_ref[0], weight_ref[:part], preferred_element_type=f32)
    for y in range(1, YS):
        total = total + jnp.dot(active_ref[y], weight_ref[y * part : (y + 1) * part], preferred_element_type=f32)
    total = total.astype(bf16)
    for k in range(out_ref.shape[0]):
        out_ref[k] = total


def local(hidden_in, queries, kv_cache, new_kv, lengths, out_weight, norm_gain, gate_weight, up_weight, down_weight):
    group, head = queries.shape[2:]
    rows = hidden_in.shape[0] * 2
    cols = hidden_in.shape[2]
    width = out_weight.shape[0]
    part = gate_weight.shape[1] // YS
    step = rows // ZS
    shape = jax.ShapeDtypeStruct

    own, hidden, gain = pl.pallas_call(
        attention_kernel,
        out_shape=[shape((2, width + LANES), bf16), shape((rows, cols), bf16), shape((1, cols), f32)],
        in_specs=[pl.BlockSpec(memory_space=pltpu.SMEM)] + [pl.BlockSpec(memory_space=pltpu.HBM)] * 5,
        out_specs=vmem(3),
        scratch_shapes=[
            pltpu.VMEM((2 * group, head), bf16),
            pltpu.VMEM((kv_cache.shape[1], 2 * head), bf16),
            pltpu.VMEM((2, 2 * head), bf16),
            pltpu.SemaphoreType.DMA((5,)),
        ],
        name="attention",
        compiler_params=SMALL,
    )(
        lengths,
        *(
            pltpu.with_memory_space_constraint(value, pltpu.HBM)
            for value in (
                queries.reshape(2 * group, head),
                kv_cache.reshape(-1, 2 * head),
                new_kv.reshape(2, 2 * head),
                hidden_in.reshape(rows, cols),
                norm_gain.reshape(1, cols),
            )
        ),
    )
    along_z = spread(own, Z, ZS).reshape(2 * ZS, width + LANES)
    everyone = spread(along_z, Y, YS).reshape(SIDES, rows, width + LANES)
    head_parts = pl.pallas_call(
        functools.partial(project_kernel, group),
        out_shape=shape((GYS, rows, cols), bf16),
        in_specs=vmem(2),
        out_specs=vmem(1)[0],
        name="project",
        compiler_params=SMALL,
    )(everyone, out_weight)
    head_parts = lax.all_to_all(head_parts, GY, 0, 0)
    middle, terms = pl.pallas_call(
        gate_kernel,
        out_shape=[shape((rows, cols), f32), shape((YS * ZP, TALL, 2 * part * (rows // ZP // TALL) + LANES), bf16)],
        in_specs=vmem(5),
        out_specs=vmem(2),
        name="gate_up",
        compiler_params=SMALL,
    )(head_parts, hidden, gain, gate_weight, up_weight)
    terms = lax.all_to_all(terms, NEAR, 0, 0)
    terms = pl.pallas_call(
        sum_kernel,
        out_shape=shape((ZQ, step, 2 * part + LANES), bf16),
        in_specs=vmem(1),
        out_specs=vmem(1)[0],
        name="near_sum",
        compiler_params=SMALL,
    )(terms)
    terms = lax.all_to_all(terms, "zq", 0, 0)
    activated = pl.pallas_call(
        activate_kernel,
        out_shape=shape((ZS, step, part), bf16),
        in_specs=vmem(1),
        out_specs=vmem(1)[0],
        name="activate",
        compiler_params=SMALL,
    )(terms)
    along_z = lax.all_to_all(activated, Z, 0, 0).reshape(rows, part)
    along_y = spread(along_z, Y, YS)
    ffn_parts = pl.pallas_call(
        down_kernel,
        out_shape=shape((GYS, rows, cols), bf16),
        in_specs=vmem(2),
        out_specs=vmem(1)[0],
        name="down",
        compiler_params=SMALL,
    )(along_y, down_weight)
    ffn_sum = jnp.sum(lax.all_to_all(ffn_parts, GY, 0, 0).astype(f32), axis=0)
    return (middle + ffn_sum).astype(bf16).reshape(hidden_in.shape)


def solution(mesh):
    fine = Mesh(mesh.devices.reshape(2, 2, ZQ, ZP, 4, 2), ("side", "yhi", "zq", "zp", "x", "core"))
    requests = ("yhi", "zq", "zp")
    in_specs = (
        P(None, None, ROWS),
        P(requests, None, GY, None),
        P(requests, "side", GY, None),
        P(requests, None, GY, None),
        P(requests),
        P(GY, ROWS),
        P(ROWS),
        P(ROWS, GY),
        P(ROWS, GY),
        P(GY, ROWS),
    )
    return jax.shard_map(local, mesh=fine, in_specs=in_specs, out_specs=P(None, None, ROWS), check_vma=False)
```

```python
import functools
import math

import jax
import jax.numpy as jnp
from jax import lax
from jax.experimental import pallas as pl
from jax.experimental.pallas import tpu as pltpu
from jax.sharding import Mesh, PartitionSpec as P

D = 8192
EPS = 1e-05
big_negative = -1e30
bf16 = jnp.bfloat16
f32 = jnp.float32

LANES, TALL = 128, 8
SIDES, YS, ZQ, ZP = 2, 4, 8, 2
ZS = ZQ * ZP
ROWS = ("side", "yhi", "zq", "zp")
Y = ("side", "yhi")
Z = ("zq", "zp")
NEAR = ("side", "yhi", "zp")
GY = ("x", "core")
GYS = 8


def order_far():
    return [0, 4, 2, 6, 1, 5, 3, 7]


def exchange_far(value):
    return lax.all_to_all(value, "zq", 0, 0, axis_index_groups=[order_far()])


def exchange_z(value):
    return lax.all_to_all(value, Z, 0, 0, axis_index_groups=[[q * ZP + p for q in order_far() for p in range(ZP)]])


def spread(value, axes, count):
    return lax.all_to_all(jnp.broadcast_to(value, (count, *value.shape)), axes, 0, 0)


SMALL = pltpu.CompilerParams(vmem_limit_bytes=12 * 2**20)


def vmem(count):
    return [pl.BlockSpec(memory_space=pltpu.VMEM)] * count


def split(total):
    high = total.astype(bf16).astype(f32)
    return high, total - high


def attention_kernel(
    length_ref,
    query_hbm,
    cache_hbm,
    fresh_hbm,
    hidden_hbm,
    gain_hbm,
    out_ref,
    hidden_ref,
    gain_ref,
    query_ref,
    cache_ref,
    fresh_ref,
    arrived,
):
    moves = (
        (cache_hbm, cache_ref),
        (query_hbm, query_ref),
        (fresh_hbm, fresh_ref),
        (hidden_hbm, hidden_ref),
        (gain_hbm, gain_ref),
    )
    copies = [pltpu.make_async_copy(source, target, arrived.at[k]) for k, (source, target) in enumerate(moves)]
    for copy in copies:
        copy.start()
    for copy in copies:
        copy.wait()
    side = lax.axis_index("side")
    half, doubled = cache_ref.shape
    head = doubled // 2
    pairs = query_ref.shape[0]
    group = pairs // 2
    scale = 1.0 / math.sqrt(head)
    contract_last = (((1,), (1,)), ((), ()))
    query = query_ref[...]
    scores = lax.dot_general(query, cache_ref[:, :head], contract_last, preferred_element_type=f32) * scale
    usable = side * half + lax.broadcasted_iota(jnp.int32, (pairs, half), 1) < length_ref[0]
    scores = jnp.where(usable, scores, big_negative)
    fresh = fresh_ref[...].astype(f32)
    draft = lax.broadcasted_iota(jnp.int32, (pairs, 1), 0) // group
    wide = query.astype(f32)
    new_scores, seen = [], []
    for u in range(2):
        seen.append((draft >= u) & (side == SIDES - 1))
        score = jnp.sum(wide * fresh[u : u + 1, :head], axis=1, keepdims=True) * scale
        new_scores.append(jnp.where(seen[u], score, big_negative))
    peak = jnp.max(scores, axis=1, keepdims=True)
    peak = jnp.maximum(peak, jnp.maximum(new_scores[0], new_scores[1]))
    peak = peak.astype(bf16).astype(f32)
    weights = jnp.where(usable, jnp.exp(scores - peak), 0.0)
    total = jnp.sum(weights, axis=1, keepdims=True)
    accum = jnp.dot(weights.astype(bf16), cache_ref[:, head:], preferred_element_type=f32)
    for u in range(2):
        weight = jnp.where(seen[u], jnp.exp(new_scores[u] - peak), 0.0)
        total = total + weight
        accum = accum + weight.astype(bf16).astype(f32) * fresh[u : u + 1, head:]
    mixed = accum / total
    high, low = split(total)
    lane = lax.broadcasted_iota(jnp.int32, (pairs, LANES), 1)
    row = lax.broadcasted_iota(jnp.int32, (pairs, LANES), 0) % group
    stats = jnp.where(lane == row, peak, 0.0)
    stats = jnp.where(lane == row + group, high, stats)
    stats = jnp.where(lane == row + 2 * group, low, stats)
    stats = [jnp.sum(stats[t * group : (t + 1) * group], axis=0, keepdims=True) for t in range(2)]
    for i in range(group):
        both = jnp.concatenate([mixed[i : i + 1], mixed[group + i : group + i + 1]], axis=0)
        out_ref[:, i * head : (i + 1) * head] = both.astype(bf16)
    out_ref[:, group * head :] = jnp.concatenate(stats, axis=0).astype(bf16)


def project_kernel(group, parts_ref, weight_ref, out_ref):
    width = weight_ref.shape[0]
    head = width // group
    stats = [parts_ref[s, :, width:].astype(f32) for s in range(SIDES)]
    totals = [stat[:, group : 2 * group] + stat[:, 2 * group : 3 * group] for stat in stats]
    peaks = [stat[:, :group] for stat in stats]
    peak = jnp.maximum(peaks[0], peaks[1])
    shares = [totals[s] * jnp.exp(peaks[s] - peak) for s in range(SIDES)]
    whole = shares[0] + shares[1]
    shares = [share / whole for share in shares]
    merged = []
    for i in range(group):
        columns = slice(i * head, (i + 1) * head)
        value = parts_ref[0, :, columns].astype(f32) * shares[0][:, i : i + 1]
        value = value + parts_ref[1, :, columns].astype(f32) * shares[1][:, i : i + 1]
        merged.append(value.astype(bf16))
    total = jnp.dot(jnp.concatenate(merged, axis=1), weight_ref[...], preferred_element_type=f32).astype(bf16)
    for k in range(out_ref.shape[0]):
        out_ref[k] = total


def gate_kernel(parts_ref, hidden_ref, gain_ref, gate_ref, up_ref, middle_ref, out_ref):
    middle = hidden_ref[...].astype(f32)
    for k in range(parts_ref.shape[0]):
        middle = middle + parts_ref[k].astype(f32)
    middle_ref[...] = middle
    rows = middle.shape[0]
    step = rows // ZS
    high, low = split(jnp.sum(middle * middle, axis=1, keepdims=True))
    scaled = middle * gain_ref[...]

    def regroup(value):
        pieces = [value[(q * ZP + p) * step : (q * ZP + p + 1) * step] for p in range(ZP) for q in range(ZQ)]
        return jnp.concatenate(pieces, axis=0)

    scaled, high, low = regroup(scaled).astype(bf16), regroup(high), regroup(low)
    part = gate_ref.shape[1] // YS
    tall = out_ref.shape[1]
    count = rows // ZP // tall
    lane = lax.broadcasted_iota(jnp.int32, (tall, LANES), 1)
    for p in range(ZP):
        stats = jnp.zeros((tall, LANES), f32)
        for g in range(count):
            block = slice((p * count + g) * tall, (p * count + g + 1) * tall)
            stats = jnp.where(lane == 2 * g, high[block], jnp.where(lane == 2 * g + 1, low[block], stats))
        for y in range(YS):
            out_ref[y * ZP + p, :, 2 * part * count :] = stats.astype(bf16)
    for y in range(YS):
        columns = slice(y * part, (y + 1) * part)
        for start, ref in ((0, gate_ref), (part, up_ref)):
            term = jnp.dot(scaled, ref[:, columns], preferred_element_type=f32)
            for p in range(ZP):
                for g in range(count):
                    block = term[(p * count + g) * tall : (p * count + g + 1) * tall].astype(bf16)
                    out_ref[y * ZP + p, :, 2 * part * g + start : 2 * part * g + start + part] = block


def sum_kernel(parts_ref, out_ref):
    total = parts_ref[0].astype(f32)
    for k in range(1, parts_ref.shape[0]):
        total = total + parts_ref[k].astype(f32)
    step = out_ref.shape[1]
    width = out_ref.shape[2] - LANES
    tall = total.shape[0]
    each = tall // step
    count = out_ref.shape[0] // each
    lane = lax.broadcasted_iota(jnp.int32, (tall, LANES), 1)
    pairs = total[:, width * count :]
    for g in range(count):
        high, low = split(pairs[:, 2 * g : 2 * g + 1] + pairs[:, 2 * g + 1 : 2 * g + 2])
        stats = jnp.where(lane == 0, high, jnp.where(lane == 1, low, 0.0))
        for e in range(each):
            rows = slice(e * step, (e + 1) * step)
            out_ref[g * each + e, :, :width] = total[rows, g * width : (g + 1) * width].astype(bf16)
            out_ref[g * each + e, :, width:] = stats[rows].astype(bf16)


def activate_kernel(parts_ref, out_ref):
    total = parts_ref[0].astype(f32)
    for k in range(1, parts_ref.shape[0]):
        total = total + parts_ref[k].astype(f32)
    part = out_ref.shape[2]
    squares = total[:, 2 * part : 2 * part + 1] + total[:, 2 * part + 1 : 2 * part + 2]
    factor = lax.rsqrt(squares / D + EPS)
    gate = total[:, :part] * factor
    up = total[:, part : 2 * part] * factor
    activated = (gate / (1.0 + jnp.exp(-gate)) * up).astype(bf16)
    for k in range(out_ref.shape[0]):
        out_ref[k] = activated


def down_kernel(active_ref, weight_ref, out_ref):
    part = active_ref.shape[2]
    total = jnp.dot(active_ref[0], weight_ref[:part], preferred_element_type=f32)
    for y in range(1, YS):
        total = total + jnp.dot(active_ref[y], weight_ref[y * part : (y + 1) * part], preferred_element_type=f32)
    total = total.astype(bf16)
    for k in range(out_ref.shape[0]):
        out_ref[k] = total


def local(hidden_in, queries, kv_cache, new_kv, lengths, out_weight, norm_gain, gate_weight, up_weight, down_weight):
    group, head = queries.shape[2:]
    rows = hidden_in.shape[0] * 2
    cols = hidden_in.shape[2]
    width = out_weight.shape[0]
    part = gate_weight.shape[1] // YS
    step = rows // ZS
    shape = jax.ShapeDtypeStruct

    own, hidden, gain = pl.pallas_call(
        attention_kernel,
        out_shape=[shape((2, width + LANES), bf16), shape((rows, cols), bf16), shape((1, cols), f32)],
        in_specs=[pl.BlockSpec(memory_space=pltpu.SMEM)] + [pl.BlockSpec(memory_space=pltpu.HBM)] * 5,
        out_specs=vmem(3),
        scratch_shapes=[
            pltpu.VMEM((2 * group, head), bf16),
            pltpu.VMEM((kv_cache.shape[1], 2 * head), bf16),
            pltpu.VMEM((2, 2 * head), bf16),
            pltpu.SemaphoreType.DMA((5,)),
        ],
        name="attention",
        compiler_params=SMALL,
    )(
        lengths,
        *(
            pltpu.with_memory_space_constraint(value, pltpu.HBM)
            for value in (
                queries.reshape(2 * group, head),
                kv_cache.reshape(-1, 2 * head),
                new_kv.reshape(2, 2 * head),
                hidden_in.reshape(rows, cols),
                norm_gain.reshape(1, cols),
            )
        ),
    )
    along_z = spread(own, Z, ZS).reshape(2 * ZS, width + LANES)
    everyone = spread(along_z, Y, YS).reshape(SIDES, rows, width + LANES)
    head_parts = pl.pallas_call(
        functools.partial(project_kernel, group),
        out_shape=shape((GYS, rows, cols), bf16),
        in_specs=vmem(2),
        out_specs=vmem(1)[0],
        name="project",
        compiler_params=SMALL,
    )(everyone, out_weight)
    head_parts = lax.all_to_all(head_parts, GY, 0, 0)
    middle, terms = pl.pallas_call(
        gate_kernel,
        out_shape=[shape((rows, cols), f32), shape((YS * ZP, TALL, 2 * part * (rows // ZP // TALL) + LANES), bf16)],
        in_specs=vmem(5),
        out_specs=vmem(2),
        name="gate_up",
        compiler_params=SMALL,
    )(head_parts, hidden, gain, gate_weight, up_weight)
    terms = lax.all_to_all(terms, NEAR, 0, 0)
    terms = pl.pallas_call(
        sum_kernel,
        out_shape=shape((ZQ, step, 2 * part + LANES), bf16),
        in_specs=vmem(1),
        out_specs=vmem(1)[0],
        name="near_sum",
        compiler_params=SMALL,
    )(terms)
    terms = exchange_far(terms)
    activated = pl.pallas_call(
        activate_kernel,
        out_shape=shape((ZS, step, part), bf16),
        in_specs=vmem(1),
        out_specs=vmem(1)[0],
        name="activate",
        compiler_params=SMALL,
    )(terms)
    along_z = exchange_z(activated).reshape(rows, part)
    along_y = spread(along_z, Y, YS)
    ffn_parts = pl.pallas_call(
        down_kernel,
        out_shape=shape((GYS, rows, cols), bf16),
        in_specs=vmem(2),
        out_specs=vmem(1)[0],
        name="down",
        compiler_params=SMALL,
    )(along_y, down_weight)
    ffn_sum = jnp.sum(lax.all_to_all(ffn_parts, GY, 0, 0).astype(f32), axis=0)
    return (middle + ffn_sum).astype(bf16).reshape(hidden_in.shape)


def solution(mesh):
    fine = Mesh(mesh.devices.reshape(2, 2, ZQ, ZP, 4, 2), ("side", "yhi", "zq", "zp", "x", "core"))
    requests = ("yhi", "zq", "zp")
    in_specs = (
        P(None, None, ROWS),
        P(requests, None, GY, None),
        P(requests, "side", GY, None),
        P(requests, None, GY, None),
        P(requests),
        P(GY, ROWS),
        P(ROWS),
        P(ROWS, GY),
        P(ROWS, GY),
        P(GY, ROWS),
    )
    return jax.shard_map(local, mesh=fine, in_specs=in_specs, out_specs=P(None, None, ROWS), check_vma=False)
```

```python
import functools
import math

import jax
import jax.numpy as jnp
from jax import lax
from jax.experimental import pallas as pl
from jax.experimental.pallas import tpu as pltpu
from jax.sharding import Mesh, PartitionSpec as P

D = 8192
EPS = 1e-05
big_negative = -1e30
bf16 = jnp.bfloat16
f32 = jnp.float32

LANES, TALL = 128, 8
SIDES, YS, ZQ, ZP = 2, 4, 8, 2
ZS = ZQ * ZP
ROWS = ("side", "yhi", "zq", "zp")
Y = ("side", "yhi")
Z = ("zq", "zp")
NEAR = ("zp", "side", "yhi")
GY = ("x", "core")
GYS = 8


def order_far():
    return [0, 4, 2, 6, 1, 5, 3, 7]


def exchange_far(value):
    return lax.all_to_all(value, "zq", 0, 0, axis_index_groups=[order_far()])


def exchange_z(value):
    return lax.all_to_all(value, Z, 0, 0, axis_index_groups=[[q * ZP + p for q in order_far() for p in range(ZP)]])


def spread(value, axes, count):
    return lax.all_to_all(jnp.broadcast_to(value, (count, *value.shape)), axes, 0, 0)


SMALL = pltpu.CompilerParams(vmem_limit_bytes=12 * 2**20)


def vmem(count):
    return [pl.BlockSpec(memory_space=pltpu.VMEM)] * count


def split(total):
    high = total.astype(bf16).astype(f32)
    return high, total - high


def attention_kernel(
    length_ref,
    query_hbm,
    cache_hbm,
    fresh_hbm,
    hidden_hbm,
    gain_hbm,
    out_ref,
    hidden_ref,
    gain_ref,
    query_ref,
    cache_ref,
    fresh_ref,
    arrived,
):
    moves = (
        (cache_hbm, cache_ref),
        (query_hbm, query_ref),
        (fresh_hbm, fresh_ref),
        (hidden_hbm, hidden_ref),
        (gain_hbm, gain_ref),
    )
    copies = [pltpu.make_async_copy(source, target, arrived.at[k]) for k, (source, target) in enumerate(moves)]
    for copy in copies:
        copy.start()
    for copy in copies:
        copy.wait()
    side = lax.axis_index("side")
    half, doubled = cache_ref.shape
    head = doubled // 2
    pairs = query_ref.shape[0]
    group = pairs // 2
    scale = 1.0 / math.sqrt(head)
    contract_last = (((1,), (1,)), ((), ()))
    query = query_ref[...]
    scores = lax.dot_general(query, cache_ref[:, :head], contract_last, preferred_element_type=f32) * scale
    usable = side * half + lax.broadcasted_iota(jnp.int32, (pairs, half), 1) < length_ref[0]
    scores = jnp.where(usable, scores, big_negative)
    fresh = fresh_ref[...].astype(f32)
    draft = lax.broadcasted_iota(jnp.int32, (pairs, 1), 0) // group
    wide = query.astype(f32)
    new_scores, seen = [], []
    for u in range(2):
        seen.append((draft >= u) & (side == SIDES - 1))
        score = jnp.sum(wide * fresh[u : u + 1, :head], axis=1, keepdims=True) * scale
        new_scores.append(jnp.where(seen[u], score, big_negative))
    peak = jnp.max(scores, axis=1, keepdims=True)
    peak = jnp.maximum(peak, jnp.maximum(new_scores[0], new_scores[1]))
    peak = peak.astype(bf16).astype(f32)
    weights = jnp.where(usable, jnp.exp(scores - peak), 0.0)
    total = jnp.sum(weights, axis=1, keepdims=True)
    accum = jnp.dot(weights.astype(bf16), cache_ref[:, head:], preferred_element_type=f32)
    for u in range(2):
        weight = jnp.where(seen[u], jnp.exp(new_scores[u] - peak), 0.0)
        total = total + weight
        accum = accum + weight.astype(bf16).astype(f32) * fresh[u : u + 1, head:]
    mixed = accum / total
    high, low = split(total)
    lane = lax.broadcasted_iota(jnp.int32, (pairs, LANES), 1)
    row = lax.broadcasted_iota(jnp.int32, (pairs, LANES), 0) % group
    stats = jnp.where(lane == row, peak, 0.0)
    stats = jnp.where(lane == row + group, high, stats)
    stats = jnp.where(lane == row + 2 * group, low, stats)
    stats = [jnp.sum(stats[t * group : (t + 1) * group], axis=0, keepdims=True) for t in range(2)]
    for i in range(group):
        both = jnp.concatenate([mixed[i : i + 1], mixed[group + i : group + i + 1]], axis=0)
        out_ref[:, i * head : (i + 1) * head] = both.astype(bf16)
    out_ref[:, group * head :] = jnp.concatenate(stats, axis=0).astype(bf16)


def project_kernel(group, parts_ref, weight_ref, out_ref):
    width = weight_ref.shape[0]
    head = width // group
    stats = [parts_ref[s, :, width:].astype(f32) for s in range(SIDES)]
    totals = [stat[:, group : 2 * group] + stat[:, 2 * group : 3 * group] for stat in stats]
    peaks = [stat[:, :group] for stat in stats]
    peak = jnp.maximum(peaks[0], peaks[1])
    shares = [totals[s] * jnp.exp(peaks[s] - peak) for s in range(SIDES)]
    whole = shares[0] + shares[1]
    shares = [share / whole for share in shares]
    merged = []
    for i in range(group):
        columns = slice(i * head, (i + 1) * head)
        value = parts_ref[0, :, columns].astype(f32) * shares[0][:, i : i + 1]
        value = value + parts_ref[1, :, columns].astype(f32) * shares[1][:, i : i + 1]
        merged.append(value.astype(bf16))
    total = jnp.dot(jnp.concatenate(merged, axis=1), weight_ref[...], preferred_element_type=f32).astype(bf16)
    for k in range(out_ref.shape[0]):
        out_ref[k] = total


def gate_kernel(parts_ref, hidden_ref, gain_ref, gate_ref, up_ref, middle_ref, out_ref):
    middle = hidden_ref[...].astype(f32)
    for k in range(parts_ref.shape[0]):
        middle = middle + parts_ref[k].astype(f32)
    middle_ref[...] = middle
    rows = middle.shape[0]
    step = rows // ZS
    high, low = split(jnp.sum(middle * middle, axis=1, keepdims=True))
    scaled = middle * gain_ref[...]

    def regroup(value):
        pieces = [value[(q * ZP + p) * step : (q * ZP + p + 1) * step] for p in range(ZP) for q in range(ZQ)]
        return jnp.concatenate(pieces, axis=0)

    scaled, high, low = regroup(scaled).astype(bf16), regroup(high), regroup(low)
    part = gate_ref.shape[1] // YS
    tall = out_ref.shape[1]
    count = rows // ZP // tall
    lane = lax.broadcasted_iota(jnp.int32, (tall, LANES), 1)
    for p in range(ZP):
        stats = jnp.zeros((tall, LANES), f32)
        for g in range(count):
            block = slice((p * count + g) * tall, (p * count + g + 1) * tall)
            stats = jnp.where(lane == 2 * g, high[block], jnp.where(lane == 2 * g + 1, low[block], stats))
        for y in range(YS):
            out_ref[p * YS + y, :, 2 * part * count :] = stats.astype(bf16)
    for y in range(YS):
        columns = slice(y * part, (y + 1) * part)
        for start, ref in ((0, gate_ref), (part, up_ref)):
            term = jnp.dot(scaled, ref[:, columns], preferred_element_type=f32)
            for p in range(ZP):
                for g in range(count):
                    block = term[(p * count + g) * tall : (p * count + g + 1) * tall].astype(bf16)
                    out_ref[p * YS + y, :, 2 * part * g + start : 2 * part * g + start + part] = block


def sum_kernel(parts_ref, out_ref):
    total = parts_ref[0].astype(f32)
    for k in range(1, parts_ref.shape[0]):
        total = total + parts_ref[k].astype(f32)
    step = out_ref.shape[1]
    width = out_ref.shape[2] - LANES
    tall = total.shape[0]
    each = tall // step
    count = out_ref.shape[0] // each
    lane = lax.broadcasted_iota(jnp.int32, (tall, LANES), 1)
    pairs = total[:, width * count :]
    for g in range(count):
        high, low = split(pairs[:, 2 * g : 2 * g + 1] + pairs[:, 2 * g + 1 : 2 * g + 2])
        stats = jnp.where(lane == 0, high, jnp.where(lane == 1, low, 0.0))
        for e in range(each):
            rows = slice(e * step, (e + 1) * step)
            out_ref[g * each + e, :, :width] = total[rows, g * width : (g + 1) * width].astype(bf16)
            out_ref[g * each + e, :, width:] = stats[rows].astype(bf16)


def activate_kernel(parts_ref, out_ref):
    total = parts_ref[0].astype(f32)
    for k in range(1, parts_ref.shape[0]):
        total = total + parts_ref[k].astype(f32)
    part = out_ref.shape[2]
    squares = total[:, 2 * part : 2 * part + 1] + total[:, 2 * part + 1 : 2 * part + 2]
    factor = lax.rsqrt(squares / D + EPS)
    gate = total[:, :part] * factor
    up = total[:, part : 2 * part] * factor
    activated = (gate / (1.0 + jnp.exp(-gate)) * up).astype(bf16)
    for k in range(out_ref.shape[0]):
        out_ref[k] = activated


def down_kernel(active_ref, weight_ref, out_ref):
    part = active_ref.shape[2]
    total = jnp.dot(active_ref[0], weight_ref[:part], preferred_element_type=f32)
    for y in range(1, YS):
        total = total + jnp.dot(active_ref[y], weight_ref[y * part : (y + 1) * part], preferred_element_type=f32)
    total = total.astype(bf16)
    for k in range(out_ref.shape[0]):
        out_ref[k] = total


def local(hidden_in, queries, kv_cache, new_kv, lengths, out_weight, norm_gain, gate_weight, up_weight, down_weight):
    group, head = queries.shape[2:]
    rows = hidden_in.shape[0] * 2
    cols = hidden_in.shape[2]
    width = out_weight.shape[0]
    part = gate_weight.shape[1] // YS
    step = rows // ZS
    shape = jax.ShapeDtypeStruct

    own, hidden, gain = pl.pallas_call(
        attention_kernel,
        out_shape=[shape((2, width + LANES), bf16), shape((rows, cols), bf16), shape((1, cols), f32)],
        in_specs=[pl.BlockSpec(memory_space=pltpu.SMEM)] + [pl.BlockSpec(memory_space=pltpu.HBM)] * 5,
        out_specs=vmem(3),
        scratch_shapes=[
            pltpu.VMEM((2 * group, head), bf16),
            pltpu.VMEM((kv_cache.shape[1], 2 * head), bf16),
            pltpu.VMEM((2, 2 * head), bf16),
            pltpu.SemaphoreType.DMA((5,)),
        ],
        name="attention",
        compiler_params=SMALL,
    )(
        lengths,
        *(
            pltpu.with_memory_space_constraint(value, pltpu.HBM)
            for value in (
                queries.reshape(2 * group, head),
                kv_cache.reshape(-1, 2 * head),
                new_kv.reshape(2, 2 * head),
                hidden_in.reshape(rows, cols),
                norm_gain.reshape(1, cols),
            )
        ),
    )
    along_z = spread(own, Z, ZS).reshape(2 * ZS, width + LANES)
    everyone = spread(along_z, Y, YS).reshape(SIDES, rows, width + LANES)
    head_parts = pl.pallas_call(
        functools.partial(project_kernel, group),
        out_shape=shape((GYS, rows, cols), bf16),
        in_specs=vmem(2),
        out_specs=vmem(1)[0],
        name="project",
        compiler_params=SMALL,
    )(everyone, out_weight)
    head_parts = lax.all_to_all(head_parts, GY, 0, 0)
    middle, terms = pl.pallas_call(
        gate_kernel,
        out_shape=[shape((rows, cols), f32), shape((YS * ZP, TALL, 2 * part * (rows // ZP // TALL) + LANES), bf16)],
        in_specs=vmem(5),
        out_specs=vmem(2),
        name="gate_up",
        compiler_params=SMALL,
    )(head_parts, hidden, gain, gate_weight, up_weight)
    terms = lax.all_to_all(terms, NEAR, 0, 0)
    terms = pl.pallas_call(
        sum_kernel,
        out_shape=shape((ZQ, step, 2 * part + LANES), bf16),
        in_specs=vmem(1),
        out_specs=vmem(1)[0],
        name="near_sum",
        compiler_params=SMALL,
    )(terms)
    terms = exchange_far(terms)
    activated = pl.pallas_call(
        activate_kernel,
        out_shape=shape((ZS, step, part), bf16),
        in_specs=vmem(1),
        out_specs=vmem(1)[0],
        name="activate",
        compiler_params=SMALL,
    )(terms)
    along_z = exchange_z(activated).reshape(rows, part)
    along_y = spread(along_z, Y, YS)
    ffn_parts = pl.pallas_call(
        down_kernel,
        out_shape=shape((GYS, rows, cols), bf16),
        in_specs=vmem(2),
        out_specs=vmem(1)[0],
        name="down",
        compiler_params=SMALL,
    )(along_y, down_weight)
    ffn_sum = jnp.sum(lax.all_to_all(ffn_parts, GY, 0, 0).astype(f32), axis=0)
    return (middle + ffn_sum).astype(bf16).reshape(hidden_in.shape)


def solution(mesh):
    fine = Mesh(mesh.devices.reshape(2, 2, ZQ, ZP, 4, 2), ("side", "yhi", "zq", "zp", "x", "core"))
    requests = ("yhi", "zq", "zp")
    in_specs = (
        P(None, None, ROWS),
        P(requests, None, GY, None),
        P(requests, "side", GY, None),
        P(requests, None, GY, None),
        P(requests),
        P(GY, ROWS),
        P(ROWS),
        P(ROWS, GY),
        P(ROWS, GY),
        P(GY, ROWS),
    )
    return jax.shard_map(local, mesh=fine, in_specs=in_specs, out_specs=P(None, None, ROWS), check_vma=False)
```
